32 devices in a mesh: gx: 4 (over y, x), gy: 8 (over z, core).
Axes of the slice: x: 2, y: 2, z: 4, core: 2. Of those that a mesh axis runs over, the one named last changes fastest.
Arguments:
- tokens: bfloat16 [512, 2048], P('gy', 'gx'), may hold values from -6 to 6
- gain: bfloat16 [2048], P('gx'), may hold values from 0.5 to 1.5
- w_router: bfloat16 [2048, 8], P('gx'), may hold values from -0.25 to 0.25
- expert_query_weight: bfloat16 [8, 2048, 16, 128], P(None, 'gx', 'gy'), may hold values from -0.25 to 0.25
- key_value_weight: bfloat16 [2048, 16, 256], P('gx', 'gy'), may hold values from -0.125 to 0.125
- expert_output_weight: bfloat16 [8, 16, 128, 2048], P(None, 'gy', None, 'gx'), may hold values from -0.25 to 0.25
- cache_keys: bfloat16 [4, 16, 4096, 128], P('gx', 'gy'), may hold values from -1220 to 1220
- cached_value_slots: bfloat16 [4, 16, 4096, 128], P('gx', 'gy'), may hold values from -6 to 6
- lengths: int32 [4], replicated, may hold values from 1 to 4096, 10240 in all
- deal: int32 [4], replicated, may hold values from 0 to 3, each once
- route: int32 [512, 2], replicated, may hold values from 0 to 7, all different within a row
Outputs:
- mixed: bfloat16 [512, 2048], P('gy', 'gx')
The draws below stay inside these ranges and needn't reach their ends.
Inputs may be any that keep to these rules, and one draw needn't show every extreme that they name: `lengths`: each request's cache holds between 1 and 4096 keys, and the longest holds exactly 4096. deal[r] is the cache slot of request r; every slot is used once. `route`: each token names 2 different attention experts.
All inputs are finite; a program needn't handle non-finite values.
Results may differ from the reference program's by a relative error of at most 0.01.
The reference program's roundings to bfloat16 on the way count: a program that leaves them out, or rounds other values in their place, can miss the bound.
Values may be sent and summed in bfloat16 or wider, within the bound.
A program may use at most 64 MiB of HBM per device.

```python
import math
import jax
import jax.numpy as jnp
import numpy as np
from jax import lax

MODEL_WIDTH = 2048
KEY_VALUE_HEADS = 16
HEAD_SIZE = 128
ATTENTION_EXPERTS = 8
EXPERTS_PER_TOKEN = 2
REQUEST_TOKENS = 128
CACHE_LENGTH = 4096
REQUEST_COUNT = 4
TOKEN_COUNT = 512


def draw_cache_keys(key, part):
    cache_offset = jax.random.normal(jax.random.fold_in(key, 11), (REQUEST_COUNT, KEY_VALUE_HEADS, CACHE_LENGTH, HEAD_SIZE), jnp.float32)
    cache_offset = jnp.clip(cache_offset, -6.0, 6.0)
    return cache_offset.astype(jnp.bfloat16)


def shard_levels(own_key, extent, split, low, largest):
    level, own = 1.0, jax.random.fold_in(own_key, 6)
    for position, blocks in split:
        steps = jnp.exp(jax.random.uniform(jax.random.fold_in(own, position), (blocks,), jnp.float32, low / len(split), largest / len(split)))
        level = level * jnp.repeat(steps, extent[position] // blocks).reshape([-1 if axis == position else 1 for axis in range(len(extent))])
    return level


def picks_of(stream_key, rows, number_of, top, lift):
    sequence = jax.random.permutation(jax.random.fold_in(stream_key, 1), number_of)
    boost = sequence
    for power in range(3):
        boost = boost * boost // number_of
    boost = boost * lift // number_of
    chance = jax.random.randint(jax.random.fold_in(stream_key, 2), (rows, number_of), 0, 4096) + boost
    sure = jax.random.permutation(jax.random.fold_in(stream_key, 3), rows)[jnp.arange(number_of) % rows]
    chance = jnp.where(jnp.arange(rows)[:, None] == sure[None, :], 1 << 14, chance)
    score = chance * number_of + jnp.arange(number_of)
    return lax.top_k(score.astype(jnp.int32), top)[1].astype(jnp.int32)


def length_profile(number_of, total, bound, lean):
    portions = [(1 << 20) // math.isqrt(rank ** lean) + 1 for rank in range(2, number_of + 1)]
    spare, holding = total - bound - (number_of - 1), [1] * (number_of - 1)
    while spare > 0:
        candidates = [i for i in range(number_of - 1) if holding[i] < bound]
        mass, remaining = sum([portions[i] for i in candidates]), spare
        for i in candidates:
            addition = min(bound - holding[i], max(1, remaining * portions[i] // mass), spare)
            holding[i] = holding[i] + addition
            spare = spare - addition
    return np.array([bound] + holding)


def ragged(rng, number_of, total, limit, slope):
    if number_of == 2:
        one = jax.random.randint(rng, (), max(1, total - limit), min(limit, total - 1) + 1)
        return jnp.stack([one, total - one])
    sizes = jnp.asarray(length_profile(number_of, total, limit, slope), jnp.int32)
    couples = (number_of - 1) // 2
    giver, taker = sizes[1:1 + 2 * couples:2], sizes[2:2 + 2 * couples:2]
    margin = jnp.minimum(giver - 1, limit - taker)
    passed = jax.random.randint(jax.random.fold_in(rng, 1), (couples,), 0, 1 << 20) % (margin + 1)
    sizes = sizes.at[1:1 + 2 * couples:2].set(giver - passed).at[2:2 + 2 * couples:2].set(taker + passed)
    return sizes[jax.random.permutation(jax.random.fold_in(rng, 2), number_of)]


def scatter_about(key, extent, spread, limit, split=(), held_as=jnp.bfloat16):
    result = jax.random.normal(key, extent, jnp.float32) * spread
    if len(split) > 0:
        result = shard_levels(key, extent, split, -0.22, 0.18) * result
    return jnp.clip(result, min=-limit, max=limit).astype(held_as)


def setup_inputs(seed: int = 0) -> dict:
    key_of = jax.random.split(jax.random.key(seed), 12)
    tokens = scatter_about(key_of[0], (TOKEN_COUNT, MODEL_WIDTH), 1.0, 6.0, ((0, 8), (1, 4)))
    gain = jnp.clip(1.0 + 0.1 * jax.random.normal(key_of[1], (MODEL_WIDTH,), jnp.float32), 0.5, 1.5).astype(jnp.bfloat16)
    w_router = scatter_about(key_of[2], (MODEL_WIDTH, ATTENTION_EXPERTS), (MODEL_WIDTH // 4) ** -0.5, 0.25, ((0, 4),))
    expert_query_weight = scatter_about(key_of[3], (ATTENTION_EXPERTS, MODEL_WIDTH, KEY_VALUE_HEADS, HEAD_SIZE), (MODEL_WIDTH // 4) ** -0.5, 0.25, ((1, 4), (2, 8)))
    key_value_weight = scatter_about(key_of[4], (MODEL_WIDTH, KEY_VALUE_HEADS, 2 * HEAD_SIZE), MODEL_WIDTH ** -0.5, 0.125, ((0, 4), (1, 8)))
    expert_output_weight = scatter_about(key_of[5], (ATTENTION_EXPERTS, KEY_VALUE_HEADS, HEAD_SIZE, MODEL_WIDTH), (HEAD_SIZE * 4) ** -0.5, 0.25, ((1, 8), (3, 4)))
    cache_keys = draw_cache_keys(jax.random.fold_in(key_of[11], 71), 0)
    cached_value_slots = scatter_about(key_of[7], (REQUEST_COUNT, KEY_VALUE_HEADS, CACHE_LENGTH, HEAD_SIZE), 1.0, 6.0, ((0, 4), (1, 8)))
    lengths = ragged(key_of[8], REQUEST_COUNT, (REQUEST_COUNT + 1) * CACHE_LENGTH // 2, CACHE_LENGTH, 1).astype(jnp.int32)
    deal = jax.random.permutation(key_of[9], REQUEST_COUNT).astype(jnp.int32)
    route = picks_of(key_of[10], TOKEN_COUNT, ATTENTION_EXPERTS, EXPERTS_PER_TOKEN, 2048)
    return {"tokens": tokens, "gain": gain, "w_router": w_router, "expert_query_weight": expert_query_weight, "key_value_weight": key_value_weight, "expert_output_weight": expert_output_weight, "cache_keys": cache_keys, "cached_value_slots": cached_value_slots, "lengths": lengths, "deal": deal, "route": route}


masked_score = -1e+30
norm_eps = 1e-06

def attend_head(operand_set, length):
    query_by_head, cache_k, cache_v, fresh_k, fresh_v = operand_set
    keys = jnp.concatenate([cache_k, fresh_k], axis=0)
    values = jnp.concatenate([cache_v, fresh_v], axis=0)
    scores = jnp.dot(query_by_head, keys.T, preferred_element_type=jnp.float32) * HEAD_SIZE ** (-0.5)
    query_rows = query_by_head.shape[0]
    token_of_row = jnp.arange(query_rows, dtype=jnp.int32) // EXPERTS_PER_TOKEN
    cache_visible = jnp.broadcast_to(jnp.arange(CACHE_LENGTH, dtype=jnp.int32)[None, :] < length, (query_rows, CACHE_LENGTH))
    fresh_visible = jnp.arange(REQUEST_TOKENS, dtype=jnp.int32)[None, :] <= token_of_row[:, None]
    visible = jnp.concatenate([cache_visible, fresh_visible], axis=1)
    scores = jnp.where(visible, scores, masked_score)
    weights = jnp.exp(scores - lax.optimization_barrier(jnp.max(scores, axis=1, keepdims=True)))
    denominator = lax.optimization_barrier(jnp.sum(weights, axis=1, keepdims=True))
    summed = jnp.dot(weights.astype(jnp.bfloat16), values, preferred_element_type=jnp.float32)
    return (summed / denominator).astype(jnp.bfloat16)

def reference(tokens, gain, w_router, expert_query_weight, key_value_weight, expert_output_weight, cache_keys, cached_value_slots, lengths, deal, route):
    widened = tokens.astype(jnp.float32)
    inverse_root_mean = lax.rsqrt(lax.optimization_barrier(jnp.mean(widened * widened, axis=1)) + norm_eps)
    scaled_input = (widened * gain.astype(jnp.float32)[None, :]).astype(jnp.bfloat16)
    logits = jnp.dot(scaled_input, w_router, preferred_element_type=jnp.float32) * inverse_root_mean[:, None]
    onehot = (route[:, :, None] == jnp.arange(ATTENTION_EXPERTS, dtype=jnp.int32)[None, None, :]).astype(jnp.float32)
    chosen = lax.optimization_barrier(jnp.sum(onehot * logits[:, None, :], axis=2))
    gate_gap = chosen[:, 0] - chosen[:, 1]
    gate_weights = jnp.stack([jax.nn.sigmoid(gate_gap), jax.nn.sigmoid(-gate_gap)], axis=1).astype(jnp.bfloat16)
    flattened_query = expert_query_weight.reshape(ATTENTION_EXPERTS, MODEL_WIDTH, KEY_VALUE_HEADS * HEAD_SIZE)
    query_totals = jnp.zeros((TOKEN_COUNT, EXPERTS_PER_TOKEN, KEY_VALUE_HEADS * HEAD_SIZE), jnp.float32)
    for expert_index in range(ATTENTION_EXPERTS):
        projected = jnp.dot(scaled_input, flattened_query[expert_index], preferred_element_type=jnp.float32)
        query_totals = query_totals + onehot[:, :, expert_index][:, :, None] * projected[:, None, :]
    query_matrix = (query_totals * inverse_root_mean[:, None, None]).astype(jnp.bfloat16).reshape(TOKEN_COUNT, EXPERTS_PER_TOKEN, KEY_VALUE_HEADS, HEAD_SIZE)
    key_value_rows = jnp.dot(scaled_input, key_value_weight.reshape(MODEL_WIDTH, KEY_VALUE_HEADS * 2 * HEAD_SIZE), preferred_element_type=jnp.float32)
    key_value_rows = (key_value_rows * inverse_root_mean[:, None]).astype(jnp.bfloat16).reshape(TOKEN_COUNT, KEY_VALUE_HEADS, 2 * HEAD_SIZE)
    expert_parts = []
    for request in range(REQUEST_COUNT):
        request_token_rows = slice(request * REQUEST_TOKENS, (request + 1) * REQUEST_TOKENS)
        cache_slot = deal[request]
        length = lengths[request]
        query_by_head = jnp.transpose(query_matrix[request_token_rows], (2, 0, 1, 3)).reshape(KEY_VALUE_HEADS, REQUEST_TOKENS * EXPERTS_PER_TOKEN, HEAD_SIZE)
        fresh_keyval = jnp.transpose(key_value_rows[request_token_rows], (1, 0, 2))
        operand_set = (query_by_head, cache_keys[cache_slot], cached_value_slots[cache_slot], fresh_keyval[:, :, :HEAD_SIZE], fresh_keyval[:, :, HEAD_SIZE:])
        layer_output = lax.map(lambda member: attend_head(member, length), operand_set)
        expert_parts.append(jnp.transpose(layer_output.reshape(KEY_VALUE_HEADS, REQUEST_TOKENS, EXPERTS_PER_TOKEN, HEAD_SIZE), (1, 2, 0, 3)))
    attended_output = jnp.concatenate(expert_parts, axis=0).reshape(TOKEN_COUNT * EXPERTS_PER_TOKEN, KEY_VALUE_HEADS * HEAD_SIZE)
    mixing = onehot * gate_weights.astype(jnp.float32)[:, :, None]
    output_sum = jnp.zeros((TOKEN_COUNT, MODEL_WIDTH), jnp.float32)
    for expert_index in range(ATTENTION_EXPERTS):
        expert_output = jnp.dot(attended_output, expert_output_weight[expert_index].reshape(KEY_VALUE_HEADS * HEAD_SIZE, MODEL_WIDTH), preferred_element_type=jnp.float32).reshape(TOKEN_COUNT, EXPERTS_PER_TOKEN, MODEL_WIDTH)
        output_sum = output_sum + lax.optimization_barrier(jnp.sum(mixing[:, :, expert_index][:, :, None] * expert_output, axis=1))
    return output_sum.astype(jnp.bfloat16)
```

```python
import functools
import math

import jax
import jax.numpy as jnp
from jax import lax
from jax.experimental import pallas as pl
from jax.experimental.pallas import tpu as pltpu
from jax.sharding import PartitionSpec as P

MESH = pl.DeviceIdType.MESH
masked_score = -1e30
norm_eps = 1e-06


def kernel(
    nx, ny, full_width,
    tokens_ref, gain_ref, wr_ref, route_ref, lengths_ref, deal_ref,
    wq_hbm, wkv_hbm, wo_hbm, k_hbm, v_hbm,
    out_ref,
    xg, wq, wkv, wo, kc, vc,
    qsend, qrecv, gsend, grecv, kvsend, kvrecv, tile, gall,
    qmat, scores, maxes, fkey, fval, agbuf, outs, psend, precv, zsend, zrecv,
    ld_sem, a_send, a_recv, f_send, q_send, q_recv, g_send, g_recv, kv_send, kv_recv,
    t_send, t_recv, at_send, at_recv, p_send, p_recv, z_send, z_recv,
):
    f32, bf16 = jnp.float32, jnp.bfloat16
    mx, my = lax.axis_index("gx"), lax.axis_index("gy")
    nz = ny // 2
    mz, core = my // 2, lax.rem(my, 2)
    partner = my + 1 - 2 * core
    tb = tokens_ref.shape[0]
    experts = wq.shape[0]
    heads, cache, hd = kc.shape
    new = xg.shape[0] // nx
    rows = 2 * new
    per_req = new // tb

    def remote(src, dst, ss, rs, dev):
        return pltpu.make_async_remote_copy(
            src_ref=src, dst_ref=dst, send_sem=ss, recv_sem=rs, device_id=dev, device_id_type=MESH
        )

    def atx(c):
        return (c, my)

    def aty(c):
        return (mx, c)

    loads = [
        pltpu.make_async_copy(s, d, ld_sem.at[i])
        for i, (s, d) in enumerate(
            ((wq_hbm, wq), (wkv_hbm, wkv), (k_hbm, kc), (v_hbm, vc), (wo_hbm, wo))
        )
    ]
    for load in loads:
        load.start()

    barrier = pltpu.get_barrier_semaphore()
    for d in range(1, nx):
        pl.semaphore_signal(barrier, inc=1, device_id=atx(lax.rem(mx + d, nx)), device_id_type=MESH)
    pl.semaphore_signal(barrier, inc=1, device_id=aty(partner), device_id_type=MESH)
    for d in range(1, nz):
        pl.semaphore_signal(
            barrier, inc=1, device_id=aty(lax.rem(mz + d, nz) * 2 + core), device_id_type=MESH
        )
    pl.semaphore_wait(barrier, nx - 1 + nz)

    def block(b):
        return xg.at[pl.ds(pl.multiple_of(b * tb, tb), tb)]

    def a_copy(d):
        return remote(tokens_ref, block(my), a_send.at[d], a_recv.at[my],
                      aty(lax.rem(mz + d, nz) * 2 + core))

    def a_in(b, ss):
        return remote(block(b), block(b), ss, a_recv.at[b], aty(partner))

    for d in range(1, nz):
        a_copy(d).start()
    own = remote(tokens_ref, block(my), a_send.at[0], a_recv.at[my], aty(partner))
    own.start()
    block(my)[...] = tokens_ref[...]
    for d in range(1, nz):
        b = lax.rem(mz + nz - d, nz) * 2 + core
        c = a_in(b, f_send.at[d])
        c.wait_recv()
        c.start()
    a_in(partner, f_send.at[0]).wait_recv()
    for d in range(1, nz):
        b = lax.rem(mz + nz - d, nz) * 2 + 1 - core
        a_in(b, f_send.at[d]).wait_recv()

    def pick(keys, wanted, values, shape):
        acc = values(0)
        for i in range(1, nx):
            acc = jnp.where(jnp.full(shape, keys(i) - wanted) == 0, values(i), acc)
        return acc

    def deal_of(i):
        return deal_ref[i]

    def route_of(c):
        return pick(deal_of, c, lambda i: route_ref[i * new:(i + 1) * new, :], (1, route_ref.shape[1]))

    tile[...] = jnp.zeros_like(tile)
    gain = gain_ref[...].astype(f32)
    loads[0].wait()

    def scaled_of(c):
        x = pick(deal_of, c, lambda i: xg[i * new:(i + 1) * new, :].astype(f32), (1, xg.shape[1]))
        return x, (x * gain).astype(bf16)

    def q_copy(c, d):
        return remote(qsend.at[d], qrecv.at[mx], q_send.at[d], q_recv.at[mx], atx(c))

    def g_copy(c, d):
        return remote(gsend.at[d], grecv.at[mx], g_send.at[d], g_recv.at[mx], atx(c))

    def kv_copy(c, d):
        return remote(kvsend.at[d], kvrecv.at[mx], kv_send.at[d], kv_recv.at[mx], atx(c))

    def project(c):
        x, xs = scaled_of(c)
        route = route_of(c)
        r0, r1 = route[:, 0:1], route[:, 1:2]
        q0 = jnp.zeros((new, heads * hd), f32)
        q1 = q0
        for e in range(experts):
            y = jnp.dot(xs, wq[e], preferred_element_type=f32)
            q0 = jnp.where(r0 == e, y, q0)
            q1 = jnp.where(r1 == e, y, q1)
        tile[:, 0:experts] = jnp.dot(xs, wr_ref[...], preferred_element_type=f32)
        tile[:, experts:experts + 1] = jnp.sum(x * x, axis=1, keepdims=True)
        return q0, q1, tile[...].T[0:16]

    def send_q(d, carry):
        c = lax.rem(mx + d, nx)
        q0, q1, g = project(c)
        qsend[d, 0:new] = q0
        qsend[d, new:rows] = q1
        gsend[d] = g
        g_copy(c, d).start()
        q_copy(c, d).start()
        return carry

    lax.fori_loop(1, nx, send_q, 0)
    q0, q1, g = project(mx)
    qsend[0, 0:new] = q0
    qsend[0, new:rows] = q1
    gsend[0] = g
    loads[1].wait()

    def send_kv(d, carry):
        c = lax.rem(mx + d, nx)
        kvsend[d] = jnp.dot(scaled_of(c)[1], wkv[...], preferred_element_type=f32)
        kv_copy(c, d).start()
        return carry

    lax.fori_loop(1, nx, send_kv, 0)
    kvsend[0] = jnp.dot(scaled_of(mx)[1], wkv[...], preferred_element_type=f32)

    for d in range(1, nx):
        c = lax.rem(mx + d, nx)
        remote(gsend.at[d], grecv.at[c], g_send.at[d], g_recv.at[c], atx(c)).wait_recv()
    g = gsend[0]
    for d in range(1, nx):
        g = g + grecv[lax.rem(mx + d, nx)]
    tile[...] = jnp.zeros_like(tile)
    tile[0:16] = g
    cols = tile[...].T
    inv = lax.rsqrt(cols[:, experts:experts + 1] * (1.0 / full_width) + norm_eps)
    inv2 = jnp.concatenate([inv, inv], axis=0)
    route = route_of(mx)
    lane = lax.broadcasted_iota(jnp.int32, (new, 128), 1)
    logits = cols * inv
    c0 = jnp.sum(jnp.where(lane == route[:, 0:1], logits, 0.0), axis=1, keepdims=True)
    c1 = jnp.sum(jnp.where(lane == route[:, 1:2], logits, 0.0), axis=1, keepdims=True)
    g0 = jax.nn.sigmoid(c0 - c1).astype(bf16).astype(f32)
    g1 = jax.nn.sigmoid(c1 - c0).astype(bf16).astype(f32)
    gall[mx] = jnp.where(lane == 0, g0, jnp.where(lane == 1, g1, 0.0)).T[0:8]

    def t_copy(d, at):
        c = lax.rem(mx + d, nx)
        return remote(gall.at[at], gall.at[at], t_send.at[d], t_recv.at[at], atx(c))

    for d in range(1, nx):
        t_copy(d, mx).start()

    for d in range(1, nx):
        c = lax.rem(mx + d, nx)
        remote(qsend.at[d], qrecv.at[c], q_send.at[d], q_recv.at[c], atx(c)).wait_recv()
    q = qsend[0]
    for d in range(1, nx):
        q = q + qrecv[lax.rem(mx + d, nx)]
    qmat[...] = (q * inv2).astype(bf16)

    bk = min(512, cache)
    length = pick(deal_of, mx, lambda i: jnp.full((1, bk), lengths_ref[i]), (1, bk))
    loads[2].wait()
    nt = (((1,), (1,)), ((), ()))
    maxes[...] = jnp.full(maxes.shape, masked_score, f32)

    def fold_max(h, s):
        m = maxes[h]
        for j in range(s.shape[1] // 128):
            m = jnp.maximum(m, s[:, j * 128:(j + 1) * 128])
        maxes[h] = m

    def score_block(i, carry):
        first = pl.multiple_of(i * bk, bk)
        visible = first + lax.broadcasted_iota(jnp.int32, (1, bk), 1) < length
        for h in range(heads):
            s = lax.dot_general(qmat[:, h * hd:(h + 1) * hd], kc[h, pl.ds(first, bk), :], nt,
                                preferred_element_type=f32)
            s = jnp.where(visible, s, masked_score)
            scores[h, :, pl.ds(first, bk)] = s
            fold_max(h, s)
        return carry

    lax.fori_loop(0, cache // bk, score_block, 0)

    for d in range(1, nx):
        c = lax.rem(mx + d, nx)
        remote(kvsend.at[d], kvrecv.at[c], kv_send.at[d], kv_recv.at[c], atx(c)).wait_recv()
    kv = kvsend[0]
    for d in range(1, nx):
        kv = kv + kvrecv[lax.rem(mx + d, nx)]
    kv = (kv * inv).astype(bf16)
    row = lax.rem(lax.broadcasted_iota(jnp.int32, (rows, new), 0), new)
    causal = lax.broadcasted_iota(jnp.int32, (rows, new), 1) <= row
    loads[3].wait()
    unit = hd ** -0.5 * math.log2(math.e)

    def at_copy(h, d, at):
        c = lax.rem(mx + d, nx)
        return remote(agbuf.at[at, h], agbuf.at[at, h], at_send.at[h, d], at_recv.at[h, at], atx(c))

    for h in range(heads):
        fkey[...] = kv[:, h * 2 * hd:h * 2 * hd + hd]
        fval[...] = kv[:, h * 2 * hd + hd:(h + 1) * 2 * hd]
        s = lax.dot_general(qmat[:, h * hd:(h + 1) * hd], fkey[...], nt, preferred_element_type=f32)
        s = jnp.where(causal, s, masked_score)
        fold_max(h, s)
        m = jnp.max(maxes[h], axis=1, keepdims=True)
        w = jnp.exp2((s - m) * unit)
        total = w
        acc = jnp.dot(w.astype(bf16), fval[...], preferred_element_type=f32)

        def weigh(i, carry, h=h, m=m):
            total, acc = carry
            first = pl.multiple_of(i * bk, bk)
            w = jnp.exp2((scores[h, :, pl.ds(first, bk)] - m) * unit)
            for j in range(bk // 128):
                total = total + w[:, j * 128:(j + 1) * 128]
            acc = acc + jnp.dot(w.astype(bf16), vc[h, pl.ds(first, bk), :], preferred_element_type=f32)
            return total, acc

        total, acc = lax.fori_loop(0, cache // bk, weigh, (total, acc))
        agbuf[mx, h] = (acc / jnp.sum(total, axis=1, keepdims=True)).astype(bf16)
        for d in range(1, nx):
            at_copy(h, d, mx).start()

    loads[4].wait()
    tile[...] = jnp.zeros_like(tile)

    def produce(c):
        route = route_of(c)
        rr = jnp.concatenate([route[:, 0:1], route[:, 1:2]], axis=0)
        tile[0:8] = gall[c]
        gate = tile[...].T
        a = [agbuf[c, h] for h in range(heads)]
        a = jnp.concatenate(a, axis=1) if heads > 1 else a[0]
        y = jnp.zeros((rows, wo.shape[2]), f32)
        for e in range(experts):
            y = y + jnp.dot(jnp.where(rr == e, a, jnp.zeros_like(a)), wo[e],
                            preferred_element_type=f32)
        outs[c] = gate[:, 0:1] * y[0:new] + gate[:, 1:2] * y[new:rows]

    produce(mx)

    def arrive(d, carry):
        c = lax.rem(mx + nx - d, nx)
        t_copy(d, c).wait_recv()
        for h in range(heads):
            at_copy(h, d, c).wait_recv()
        produce(c)
        return carry

    lax.fori_loop(1, nx, arrive, 0)

    def partial(b):
        slot = deal_ref[b // per_req]
        part = pl.ds(pl.multiple_of(lax.rem(b, per_req) * tb, tb), tb)
        return pick(lambda i: i, slot, lambda i: outs[i, part, :], (1, outs.shape[2]))

    for z in range(nz):
        psend[z] = partial(z * 2 + 1 - core)
    pc = remote(psend, precv, p_send, p_recv, aty(partner))
    pc.start()
    pc.wait_recv()

    def z_copy(d, at):
        return remote(zsend.at[d], zrecv.at[at], z_send.at[d], z_recv.at[at],
                      aty(lax.rem(mz + d, nz) * 2 + core))

    for d in range(nz - 1, 0, -1):
        z = lax.rem(mz + d, nz)
        zsend[d] = (partial(z * 2 + core) + precv[z]).astype(bf16)
        z_copy(d, mz).start()
    total = partial(my) + precv[mz]
    for d in range(1, nz):
        z = lax.rem(mz + nz - d, nz)
        z_copy(d, z).wait_recv()
        total = total + zrecv[z].astype(f32)
    out_ref[...] = total.astype(bf16)

    own.wait_send()
    for d in range(1, nz):
        a_copy(d).wait_send()
        a_in(lax.rem(mz + nz - d, nz) * 2 + core, f_send.at[d]).wait_send()
        z_copy(d, mz).wait_send()
    pc.wait_send()
    for d in range(1, nx):
        c = lax.rem(mx + d, nx)
        g_copy(c, d).wait_send()
        q_copy(c, d).wait_send()
        kv_copy(c, d).wait_send()
        t_copy(d, mx).wait_send()
        for h in range(heads):
            at_copy(h, d, mx).wait_send()


def per_device(nx, ny, tokens, gain, w_router, wq, wkv, wo, ck, cv, lengths, deal, route):
    f32, bf16 = jnp.float32, jnp.bfloat16
    tb, width = tokens.shape
    experts, _, heads, hd = wq.shape
    out_w = wo.shape[3]
    cache = ck.shape[2]
    nz = ny // 2
    total = tb * ny
    new = total // nx
    rows = 2 * new
    hw = heads * hd
    dma = pltpu.SemaphoreType.DMA
    vm = pltpu.VMEM
    vspec = pl.BlockSpec(memory_space=pltpu.VMEM)
    sspec = pl.BlockSpec(memory_space=pltpu.SMEM)
    aspec = pl.BlockSpec(memory_space=pl.ANY)
    return pl.pallas_call(
        functools.partial(kernel, nx, ny, width * nx),
        out_shape=jax.ShapeDtypeStruct((tb, out_w), bf16),
        in_specs=[vspec] * 4 + [sspec] * 2 + [aspec] * 5,
        out_specs=vspec,
        scratch_shapes=[
            vm((total, width), bf16),
            vm((experts, width, hw), bf16),
            vm((width, 2 * hw), bf16),
            vm((experts, hw, out_w), bf16),
            vm((heads, cache, hd), bf16),
            vm((heads, cache, hd), bf16),
            vm((nx, rows, hw), f32),
            vm((nx, rows, hw), f32),
            vm((nx, 16, new), f32),
            vm((nx, 16, new), f32),
            vm((nx, new, 2 * hw), f32),
            vm((nx, new, 2 * hw), f32),
            vm((new, 128), f32),
            vm((nx, 8, new), f32),
            vm((rows, hw), bf16),
            vm((heads, rows, cache), f32),
            vm((heads, rows, 128), f32),
            vm((new, hd), bf16),
            vm((new, hd), bf16),
            vm((nx, heads, rows, hd), bf16),
            vm((nx, new, out_w), f32),
            vm((nz, tb, out_w), f32),
            vm((nz, tb, out_w), f32),
            vm((nz, tb, out_w), bf16),
            vm((nz, tb, out_w), bf16),
            dma((5,)), dma((nz,)), dma((ny,)), dma((nz,)),
            dma((nx,)), dma((nx,)), dma((nx,)), dma((nx,)), dma((nx,)), dma((nx,)),
            dma((nx,)), dma((nx,)), dma((heads, nx)), dma((heads, nx)),
            dma, dma, dma((nz,)), dma((nz,)),
        ],
        compiler_params=pltpu.CompilerParams(
            collective_id=0, has_side_effects=True, vmem_limit_bytes=48 * 1024 * 1024
        ),
    )(
        tokens, gain.reshape(1, width), w_router, route, lengths, deal,
        wq.reshape(experts, width, hw), wkv.reshape(width, 2 * hw),
        wo.reshape(experts, hw, out_w), ck[0], cv[0],
    )


def solution(mesh):
    placed = (
        P("gy", "gx"), P("gx"), P("gx", None), P(None, "gx", "gy", None), P("gx", "gy", None),
        P(None, "gy", None, "gx"), P("gx", "gy", None, None), P("gx", "gy", None, None),
        P(), P(), P(),
    )
    return jax.shard_map(
        functools.partial(per_device, mesh.shape["gx"], mesh.shape["gy"]),
        mesh=mesh, in_specs=placed, out_specs=P("gy", "gx"), check_vma=False,
    )
```

```python
import functools
import math

import jax
import jax.numpy as jnp
from jax import lax
from jax.experimental import pallas as pl
from jax.experimental.pallas import tpu as pltpu
from jax.sharding import PartitionSpec as P

MESH = pl.DeviceIdType.MESH
masked_score = -1e30
norm_eps = 1e-06


def kernel(
    nx, ny, full_width,
    tokens_ref, gain_ref, wr_ref, route_ref, lengths_ref, deal_ref,
    wq_hbm, wkv_hbm, wo_hbm, k_hbm, v_hbm,
    out_ref,
    xg, wq4, wkv3, wq, wkv, wo, kc, vc, rcol,
    qsend, qrecv, gsend, grecv, kvsend, kvrecv, kvown, tile, gall,
    qmat, scores, maxes, fkey, fval, agbuf, outs, psend, precv, zsend, zrecv,
    ld_sem, a_send, a_recv, f_send, q_send, q_recv, g_send, g_recv, kv_send, kv_recv,
    t_send, t_recv, at_send, at_recv, p_send, p_recv, z_send, z_recv,
):
    f32, bf16 = jnp.float32, jnp.bfloat16
    nt = (((1,), (1,)), ((), ()))
    mx, my = lax.axis_index("gx"), lax.axis_index("gy")
    nz = ny // 2
    mz, core = my // 2, lax.rem(my, 2)
    partner = my + 1 - 2 * core
    tb = tokens_ref.shape[0]
    experts = wq.shape[0]
    heads, cache, hd = kc.shape
    new = xg.shape[0] // nx
    rows = 2 * new
    per_req = new // tb

    def remote(src, dst, ss, rs, dev):
        return pltpu.make_async_remote_copy(
            src_ref=src, dst_ref=dst, send_sem=ss, recv_sem=rs, device_id=dev, device_id_type=MESH
        )

    def atx(c):
        return (c, my)

    def aty(c):
        return (mx, c)

    loads = [
        pltpu.make_async_copy(s, d, ld_sem.at[i])
        for i, (s, d) in enumerate(
            ((wq_hbm, wq4), (wkv_hbm, wkv3), (k_hbm, kc), (v_hbm, vc), (wo_hbm, wo))
        )
    ]
    for load in loads:
        load.start()

    barrier = pltpu.get_barrier_semaphore()
    for d in range(1, nx):
        pl.semaphore_signal(barrier, inc=1, device_id=atx(lax.rem(mx + d, nx)), device_id_type=MESH)
    pl.semaphore_signal(barrier, inc=1, device_id=aty(partner), device_id_type=MESH)
    for d in range(1, nz):
        pl.semaphore_signal(
            barrier, inc=1, device_id=aty(lax.rem(mz + d, nz) * 2 + core), device_id_type=MESH
        )
    pl.semaphore_wait(barrier, nx - 1 + nz)

    def block(b):
        return xg.at[pl.ds(pl.multiple_of(b * tb, tb), tb)]

    def a_copy(d):
        return remote(tokens_ref, block(my), a_send.at[d], a_recv.at[my],
                      aty(lax.rem(mz + d, nz) * 2 + core))

    def a_in(b, ss):
        return remote(block(b), block(b), ss, a_recv.at[b], aty(partner))

    for d in range(1, nz):
        a_copy(d).start()
    own = remote(tokens_ref, block(my), a_send.at[0], a_recv.at[my], aty(partner))
    own.start()
    block(my)[...] = tokens_ref[...]
    def pick(keys, wanted, values, shape):
        acc = values(0)
        for i in range(1, nx):
            acc = jnp.where(jnp.full(shape, keys(i) - wanted) == 0, values(i), acc)
        return acc

    def deal_of(i):
        return deal_ref[i]

    def route_of(c):
        return rcol[c]

    tile[...] = jnp.zeros_like(tile)
    gain = gain_ref[...].astype(f32).reshape(1, gain_ref.shape[0])

    def route_column(c, carry):
        slots = route_ref.shape[0]
        tile[0:slots] = pick(
            deal_of, c, lambda i: route_ref[:, i * new:(i + 1) * new].astype(f32), (slots, new)
        )
        rcol[c] = tile[...].T
        return carry

    lax.fori_loop(0, nx, route_column, 0)
    loads[0].wait()

    def relayout(e, carry):
        for h in range(heads):
            wq[e, :, h * hd:(h + 1) * hd] = wq4[e, :, h, :]
        return carry

    lax.fori_loop(0, experts, relayout, 0)
    loads[1].wait()
    for h in range(heads):
        wkv[:, h * 2 * hd:(h + 1) * 2 * hd] = wkv3[:, h, :]


    for d in range(1, nz):
        b = lax.rem(mz + nz - d, nz) * 2 + core
        c = a_in(b, f_send.at[d])
        c.wait_recv()
        c.start()
    a_in(partner, f_send.at[0]).wait_recv()
    for d in range(1, nz):
        b = lax.rem(mz + nz - d, nz) * 2 + 1 - core
        a_in(b, f_send.at[d]).wait_recv()

    def scaled_of(c):
        x = pick(deal_of, c, lambda i: xg[i * new:(i + 1) * new, :].astype(f32), (1, xg.shape[1]))
        return x, (x * gain).astype(bf16)

    def q_copy(c, d):
        return remote(qsend.at[d], qrecv.at[mx], q_send.at[d], q_recv.at[mx], atx(c))

    def g_copy(c, d):
        return remote(gsend.at[d], grecv.at[mx], g_send.at[d], g_recv.at[mx], atx(c))

    def kv_copy(c, d):
        return remote(kvsend.at[d], kvrecv.at[mx], kv_send.at[d], kv_recv.at[mx], atx(c))

    def project(c):
        x, xs = scaled_of(c)
        route = route_of(c)
        r0, r1 = route[:, 0:1], route[:, 1:2]
        q0 = jnp.zeros((new, heads * hd), f32)
        q1 = q0
        for e in range(experts):
            y = jnp.dot(xs, wq[e], preferred_element_type=f32)
            q0 = jnp.where(r0 == float(e), y, q0)
            q1 = jnp.where(r1 == float(e), y, q1)
        tile[:, 0:experts] = lax.dot_general(xs, wr_ref[...], nt, preferred_element_type=f32)
        tile[:, experts:experts + 1] = jnp.sum(x * x, axis=1, keepdims=True)
        return q0, q1, tile[...].T[0:16]

    def send_q(d, carry):
        c = lax.rem(mx + d, nx)
        q0, q1, g = project(c)
        qsend[d, 0:new] = q0
        qsend[d, new:rows] = q1
        gsend[d] = g
        g_copy(c, d).start()
        q_copy(c, d).start()
        return carry

    lax.fori_loop(1, nx, send_q, 0)
    q0, q1, g = project(mx)
    qsend[0, 0:new] = q0
    qsend[0, new:rows] = q1
    gsend[0] = g
    def send_kv(d, carry):
        c = lax.rem(mx + d, nx)
        kvsend[d] = jnp.dot(scaled_of(c)[1], wkv[...], preferred_element_type=f32).astype(bf16)
        kv_copy(c, d).start()
        return carry

    lax.fori_loop(1, nx, send_kv, 0)
    kvown[...] = jnp.dot(scaled_of(mx)[1], wkv[...], preferred_element_type=f32)

    for d in range(1, nx):
        c = lax.rem(mx + d, nx)
        remote(gsend.at[d], grecv.at[c], g_send.at[d], g_recv.at[c], atx(c)).wait_recv()
    g = gsend[0]
    for d in range(1, nx):
        g = g + grecv[lax.rem(mx + d, nx)]
    tile[...] = jnp.zeros_like(tile)
    tile[0:16] = g
    cols = tile[...].T
    inv = lax.rsqrt(cols[:, experts:experts + 1] * (1.0 / full_width) + norm_eps)
    inv2 = jnp.concatenate([inv, inv], axis=0)
    route = route_of(mx)
    lane = lax.broadcasted_iota(jnp.int32, (new, 128), 1).astype(f32)
    logits = cols * inv
    c0 = jnp.sum(jnp.where(lane == route[:, 0:1], logits, 0.0), axis=1, keepdims=True)
    c1 = jnp.sum(jnp.where(lane == route[:, 1:2], logits, 0.0), axis=1, keepdims=True)
    g0 = jax.nn.sigmoid(c0 - c1).astype(bf16).astype(f32)
    g1 = jax.nn.sigmoid(c1 - c0).astype(bf16).astype(f32)
    gall[mx] = jnp.where(lane == 0, g0, jnp.where(lane == 1, g1, 0.0)).T[0:8]

    def t_copy(d, at):
        c = lax.rem(mx + d, nx)
        return remote(gall.at[at], gall.at[at], t_send.at[d], t_recv.at[at], atx(c))

    for d in range(1, nx):
        t_copy(d, mx).start()

    for d in range(1, nx):
        c = lax.rem(mx + d, nx)
        remote(qsend.at[d], qrecv.at[c], q_send.at[d], q_recv.at[c], atx(c)).wait_recv()
    q = qsend[0]
    for d in range(1, nx):
        q = q + qrecv[lax.rem(mx + d, nx)]
    qmat[...] = (q * inv2).astype(bf16)

    bk = min(512, cache)
    length = pick(deal_of, mx, lambda i: jnp.full((1, bk), lengths_ref[i]), (1, bk))
    loads[2].wait()
    maxes[...] = jnp.full(maxes.shape, masked_score, f32)

    def fold_max(h, s):
        m = maxes[h]
        for j in range(s.shape[1] // 128):
            m = jnp.maximum(m, s[:, j * 128:(j + 1) * 128])
        maxes[h] = m

    def score_block(i, carry):
        first = pl.multiple_of(i * bk, bk)
        visible = first + lax.broadcasted_iota(jnp.int32, (1, bk), 1) < length
        for h in range(heads):
            s = lax.dot_general(qmat[:, h * hd:(h + 1) * hd], kc[h, pl.ds(first, bk), :], nt,
                                preferred_element_type=f32)
            s = jnp.where(visible, s, masked_score)
            scores[h, :, pl.ds(first, bk)] = s
            fold_max(h, s)
        return carry

    lax.fori_loop(0, cache // bk, score_block, 0)

    for d in range(1, nx):
        c = lax.rem(mx + d, nx)
        remote(kvsend.at[d], kvrecv.at[c], kv_send.at[d], kv_recv.at[c], atx(c)).wait_recv()
    kv = kvown[...]
    for d in range(1, nx):
        kv = kv + kvrecv[lax.rem(mx + d, nx)].astype(f32)
    kv = (kv * inv).astype(bf16)
    row = lax.rem(lax.broadcasted_iota(jnp.int32, (rows, new), 0), new)
    causal = lax.broadcasted_iota(jnp.int32, (rows, new), 1) <= row
    loads[3].wait()
    unit = hd ** -0.5 * math.log2(math.e)

    def at_copy(h, d, at):
        c = lax.rem(mx + d, nx)
        return remote(agbuf.at[at, h], agbuf.at[at, h], at_send.at[h, d], at_recv.at[h, at], atx(c))

    for h in range(heads):
        fkey[...] = kv[:, h * 2 * hd:h * 2 * hd + hd]
        fval[...] = kv[:, h * 2 * hd + hd:(h + 1) * 2 * hd]
        s = lax.dot_general(qmat[:, h * hd:(h + 1) * hd], fkey[...], nt, preferred_element_type=f32)
        s = jnp.where(causal, s, masked_score)
        fold_max(h, s)
        m = jnp.max(maxes[h], axis=1, keepdims=True)
        w = jnp.exp2((s - m) * unit)
        total = w
        acc = jnp.dot(w.astype(bf16), fval[...], preferred_element_type=f32)

        def weigh(i, carry, h=h, m=m):
            total, acc = carry
            first = pl.multiple_of(i * bk, bk)
            w = jnp.exp2((scores[h, :, pl.ds(first, bk)] - m) * unit)
            for j in range(bk // 128):
                total = total + w[:, j * 128:(j + 1) * 128]
            acc = acc + jnp.dot(w.astype(bf16), vc[h, pl.ds(first, bk), :], preferred_element_type=f32)
            return total, acc

        total, acc = lax.fori_loop(0, cache // bk, weigh, (total, acc))
        agbuf[mx, h] = (acc / jnp.sum(total, axis=1, keepdims=True)).astype(bf16)
        for d in range(1, nx):
            at_copy(h, d, mx).start()

    loads[4].wait()
    tile[...] = jnp.zeros_like(tile)

    def produce(c):
        route = route_of(c)
        rr = jnp.concatenate([route[:, 0:1], route[:, 1:2]], axis=0)
        tile[0:8] = gall[c]
        gate = tile[...].T
        a = [agbuf[c, h] for h in range(heads)]
        a = jnp.concatenate(a, axis=1) if heads > 1 else a[0]
        spread = [jnp.where(rr == float(e), a, jnp.zeros_like(a)) for e in range(experts)]
        y = jnp.dot(jnp.concatenate(spread, axis=1), wo[...], preferred_element_type=f32)
        outs[c] = gate[:, 0:1] * y[0:new] + gate[:, 1:2] * y[new:rows]

    produce(mx)

    def arrive(d, carry):
        c = lax.rem(mx + nx - d, nx)
        t_copy(d, c).wait_recv()
        for h in range(heads):
            at_copy(h, d, c).wait_recv()
        produce(c)
        return carry

    lax.fori_loop(1, nx, arrive, 0)

    def partial(b):
        slot = deal_ref[b // per_req]
        part = pl.ds(pl.multiple_of(lax.rem(b, per_req) * tb, tb), tb)
        return pick(lambda i: i, slot, lambda i: outs[i, part, :], (1, outs.shape[2]))

    for z in range(nz):
        psend[z] = partial(z * 2 + 1 - core)
    pc = remote(psend, precv, p_send, p_recv, aty(partner))
    pc.start()
    pc.wait_recv()

    def z_copy(d, at):
        return remote(zsend.at[d], zrecv.at[at], z_send.at[d], z_recv.at[at],
                      aty(lax.rem(mz + d, nz) * 2 + core))

    for d in range(nz - 1, 0, -1):
        z = lax.rem(mz + d, nz)
        zsend[d] = (partial(z * 2 + core) + precv[z]).astype(bf16)
        z_copy(d, mz).start()
    total = partial(my) + precv[mz]
    for d in range(1, nz):
        z = lax.rem(mz + nz - d, nz)
        z_copy(d, z).wait_recv()
        total = total + zrecv[z].astype(f32)
    out_ref[...] = total.astype(bf16)

    own.wait_send()
    for d in range(1, nz):
        a_copy(d).wait_send()
        a_in(lax.rem(mz + nz - d, nz) * 2 + core, f_send.at[d]).wait_send()
        z_copy(d, mz).wait_send()
    pc.wait_send()
    for d in range(1, nx):
        c = lax.rem(mx + d, nx)
        g_copy(c, d).wait_send()
        q_copy(c, d).wait_send()
        kv_copy(c, d).wait_send()
        t_copy(d, mx).wait_send()
        for h in range(heads):
            at_copy(h, d, mx).wait_send()


def per_device(nx, ny, tokens, gain, w_router, wq, wkv, wo, ck, cv, lengths, deal, route):
    f32, bf16 = jnp.float32, jnp.bfloat16
    tb, width = tokens.shape
    experts, _, heads, hd = wq.shape
    out_w = wo.shape[3]
    cache = ck.shape[2]
    nz = ny // 2
    total = tb * ny
    new = total // nx
    rows = 2 * new
    hw = heads * hd
    dma = pltpu.SemaphoreType.DMA
    vm = pltpu.VMEM
    vspec = pl.BlockSpec(memory_space=pltpu.VMEM)
    sspec = pl.BlockSpec(memory_space=pltpu.SMEM)
    aspec = pl.BlockSpec(memory_space=pl.ANY)
    return pl.pallas_call(
        functools.partial(kernel, nx, ny, width * nx),
        out_shape=jax.ShapeDtypeStruct((tb, out_w), bf16),
        in_specs=[vspec] * 4 + [sspec] * 2 + [aspec] * 5,
        out_specs=vspec,
        scratch_shapes=[
            vm((total, width), bf16),
            vm((experts, width, heads, hd), bf16),
            vm((width, heads, 2 * hd), bf16),
            vm((experts, width, hw), bf16),
            vm((width, 2 * hw), bf16),
            vm((experts * hw, out_w), bf16),
            vm((heads, cache, hd), bf16),
            vm((heads, cache, hd), bf16),
            vm((nx, new, 128), f32),
            vm((nx, rows, hw), f32),
            vm((nx, rows, hw), f32),
            vm((nx, 16, new), f32),
            vm((nx, 16, new), f32),
            vm((nx, new, 2 * hw), bf16),
            vm((nx, new, 2 * hw), bf16),
            vm((new, 2 * hw), f32),
            vm((new, 128), f32),
            vm((nx, 8, new), f32),
            vm((rows, hw), bf16),
            vm((heads, rows, cache), f32),
            vm((heads, rows, 128), f32),
            vm((new, hd), bf16),
            vm((new, hd), bf16),
            vm((nx, heads, rows, hd), bf16),
            vm((nx, new, out_w), f32),
            vm((nz, tb, out_w), f32),
            vm((nz, tb, out_w), f32),
            vm((nz, tb, out_w), bf16),
            vm((nz, tb, out_w), bf16),
            dma((5,)), dma((nz,)), dma((ny,)), dma((nz,)),
            dma((nx,)), dma((nx,)), dma((nx,)), dma((nx,)), dma((nx,)), dma((nx,)),
            dma((nx,)), dma((nx,)), dma((heads, nx)), dma((heads, nx)),
            dma, dma, dma((nz,)), dma((nz,)),
        ],
        compiler_params=pltpu.CompilerParams(
            collective_id=0, has_side_effects=True, vmem_limit_bytes=60 * 1024 * 1024
        ),
    )(
        tokens, gain, w_router.T, route.T, lengths, deal,
        wq, wkv,
        wo.reshape(experts * hw, out_w), ck[0], cv[0],
    )


def solution(mesh):
    placed = (
        P("gy", "gx"), P("gx"), P("gx", None), P(None, "gx", "gy", None), P("gx", "gy", None),
        P(None, "gy", None, "gx"), P("gx", "gy", None, None), P("gx", "gy", None, None),
        P(), P(), P(),
    )
    return jax.shard_map(
        functools.partial(per_device, mesh.shape["gx"], mesh.shape["gy"]),
        mesh=mesh, in_specs=placed, out_specs=P("gy", "gx"), check_vma=False,
    )
```

```python
import functools
import math

import jax
import jax.numpy as jnp
from jax import lax
from jax.experimental import pallas as pl
from jax.experimental.pallas import tpu as pltpu
from jax.sharding import PartitionSpec as P

MESH = pl.DeviceIdType.MESH
masked_score = -1e30
norm_eps = 1e-06


def kernel(
    nx, ny, full_width,
    tokens_ref, gain_ref, wr_ref, route_ref, lengths_ref, deal_ref,
    wq_hbm, wkv_hbm, wo_hbm, k_hbm, v_hbm,
    out_ref,
    xg, wq4, wkv3, wq, wkv, wo, kc, vc, rcol,
    qsend, qrecv, gsend, grecv, kvsend, kvrecv, kvown, tile, gall,
    qmat, scores, maxes, fkey, fval, agbuf, outs, psend, precv, zsend, zrecv,
    ld_sem, a_send, a_recv, f_send, q_send, q_recv, g_send, g_recv, kv_send, kv_recv,
    t_send, t_recv, at_send, at_recv, p_send, p_recv, z_send, z_recv,
):
    f32, bf16 = jnp.float32, jnp.bfloat16
    nt = (((1,), (1,)), ((), ()))
    mx, my = lax.axis_index("gx"), lax.axis_index("gy")
    nz = ny // 2
    mz, core = my // 2, lax.rem(my, 2)
    partner = my + 1 - 2 * core
    tb = tokens_ref.shape[0]
    experts = wq.shape[0]
    heads, cache, hd = kc.shape
    new = xg.shape[0] // nx
    rows = 2 * new
    per_req = new // tb

    def remote(src, dst, ss, rs, dev):
        return pltpu.make_async_remote_copy(
            src_ref=src, dst_ref=dst, send_sem=ss, recv_sem=rs, device_id=dev, device_id_type=MESH
        )

    def atx(c):
        return (c, my)

    def aty(c):
        return (mx, c)

    loads = [
        pltpu.make_async_copy(s, d, ld_sem.at[i])
        for i, (s, d) in enumerate(
            ((wq_hbm, wq4), (wkv_hbm, wkv3), (k_hbm, kc), (v_hbm, vc), (wo_hbm, wo))
        )
    ]
    for load in loads:
        load.start()

    barrier = pltpu.get_barrier_semaphore()
    for d in range(1, nx):
        pl.semaphore_signal(barrier, inc=1, device_id=atx(lax.rem(mx + d, nx)), device_id_type=MESH)
    pl.semaphore_signal(barrier, inc=1, device_id=aty(partner), device_id_type=MESH)
    for d in range(1, nz):
        pl.semaphore_signal(
            barrier, inc=1, device_id=aty(lax.rem(mz + d, nz) * 2 + core), device_id_type=MESH
        )
    pl.semaphore_wait(barrier, nx - 1 + nz)

    def block(b):
        return xg.at[pl.ds(pl.multiple_of(b * tb, tb), tb)]

    def a_copy(d):
        return remote(tokens_ref, block(my), a_send.at[d], a_recv.at[my],
                      aty(lax.rem(mz + d, nz) * 2 + core))

    def a_in(b, ss):
        return remote(block(b), block(b), ss, a_recv.at[b], aty(partner))

    for d in range(1, nz):
        a_copy(d).start()
    own = remote(tokens_ref, block(my), a_send.at[0], a_recv.at[my], aty(partner))
    own.start()
    block(my)[...] = tokens_ref[...]
    def pick(keys, wanted, values, shape):
        acc = values(0)
        for i in range(1, nx):
            acc = jnp.where(jnp.full(shape, keys(i) - wanted) == 0, values(i), acc)
        return acc

    def deal_of(i):
        return deal_ref[i]

    def route_of(c):
        return rcol[c]

    tile[...] = jnp.zeros_like(tile)
    gain = gain_ref[...].astype(f32).reshape(1, gain_ref.shape[0])

    def route_column(c, carry):
        slots = route_ref.shape[0]
        tile[0:slots] = pick(
            deal_of, c, lambda i: route_ref[:, i * new:(i + 1) * new].astype(f32), (slots, new)
        )
        rcol[c] = tile[...].T
        return carry

    lax.fori_loop(0, nx, route_column, 0)
    loads[0].wait()

    def relayout(e, carry):
        for h in range(heads):
            wq[e, :, h * hd:(h + 1) * hd] = wq4[e, :, h, :]
        return carry

    lax.fori_loop(0, experts, relayout, 0)
    loads[1].wait()
    for h in range(heads):
        wkv[:, h * 2 * hd:(h + 1) * 2 * hd] = wkv3[:, h, :]


    for d in range(1, nz):
        b = lax.rem(mz + nz - d, nz) * 2 + core
        c = a_in(b, f_send.at[d])
        c.wait_recv()
        c.start()
    a_in(partner, f_send.at[0]).wait_recv()
    for d in range(1, nz):
        b = lax.rem(mz + nz - d, nz) * 2 + 1 - core
        a_in(b, f_send.at[d]).wait_recv()

    def scaled_of(c):
        x = pick(deal_of, c, lambda i: xg[i * new:(i + 1) * new, :].astype(f32), (1, xg.shape[1]))
        return x, (x * gain).astype(bf16)

    def q_copy(c, d):
        return remote(qsend.at[d], qrecv.at[mx], q_send.at[d], q_recv.at[mx], atx(c))

    def g_copy(c, d):
        return remote(gsend.at[d], grecv.at[mx], g_send.at[d], g_recv.at[mx], atx(c))

    def kv_copy(c, d):
        return remote(kvsend.at[d], kvrecv.at[mx], kv_send.at[d], kv_recv.at[mx], atx(c))

    def project(c):
        x, xs = scaled_of(c)
        route = route_of(c)
        r0, r1 = route[:, 0:1], route[:, 1:2]
        q0 = jnp.zeros((new, heads * hd), f32)
        q1 = q0
        for e in range(experts):
            y = jnp.dot(xs, wq[e], preferred_element_type=f32)
            q0 = jnp.where(r0 == float(e), y, q0)
            q1 = jnp.where(r1 == float(e), y, q1)
        tile[:, 0:experts] = lax.dot_general(xs, wr_ref[...], nt, preferred_element_type=f32)
        tile[:, experts:experts + 1] = jnp.sum(x * x, axis=1, keepdims=True)
        return q0, q1, tile[...].T[0:16]

    def send_q(d, carry):
        c = lax.rem(mx + d, nx)
        q0, q1, g = project(c)
        qsend[d, 0:new] = q0
        qsend[d, new:rows] = q1
        gsend[d] = g
        g_copy(c, d).start()
        q_copy(c, d).start()
        return carry

    lax.fori_loop(1, nx, send_q, 0)
    q0, q1, g = project(mx)
    qsend[0, 0:new] = q0
    qsend[0, new:rows] = q1
    gsend[0] = g
    def send_kv(d, carry):
        c = lax.rem(mx + d, nx)
        kvsend[d] = jnp.dot(scaled_of(c)[1], wkv[...], preferred_element_type=f32).astype(bf16)
        kv_copy(c, d).start()
        return carry

    lax.fori_loop(1, nx, send_kv, 0)
    kvown[...] = jnp.dot(scaled_of(mx)[1], wkv[...], preferred_element_type=f32)

    for d in range(1, nx):
        c = lax.rem(mx + d, nx)
        remote(gsend.at[d], grecv.at[c], g_send.at[d], g_recv.at[c], atx(c)).wait_recv()
    g = gsend[0]
    for d in range(1, nx):
        g = g + grecv[lax.rem(mx + d, nx)]
    tile[...] = jnp.zeros_like(tile)
    tile[0:16] = g
    cols = tile[...].T
    inv = lax.rsqrt(cols[:, experts:experts + 1] * (1.0 / full_width) + norm_eps)
    inv2 = jnp.concatenate([inv, inv], axis=0)
    route = route_of(mx)
    lane = lax.broadcasted_iota(jnp.int32, (new, 128), 1).astype(f32)
    logits = cols * inv
    c0 = jnp.sum(jnp.where(lane == route[:, 0:1], logits, 0.0), axis=1, keepdims=True)
    c1 = jnp.sum(jnp.where(lane == route[:, 1:2], logits, 0.0), axis=1, keepdims=True)
    g0 = jax.nn.sigmoid(c0 - c1).astype(bf16).astype(f32)
    g1 = jax.nn.sigmoid(c1 - c0).astype(bf16).astype(f32)
    gall[mx] = jnp.where(lane == 0, g0, jnp.where(lane == 1, g1, 0.0)).T[0:8]

    def t_copy(d, at):
        c = lax.rem(mx + d, nx)
        return remote(gall.at[at], gall.at[at], t_send.at[d], t_recv.at[at], atx(c))

    for d in range(1, nx):
        t_copy(d, mx).start()

    for d in range(1, nx):
        c = lax.rem(mx + d, nx)
        remote(qsend.at[d], qrecv.at[c], q_send.at[d], q_recv.at[c], atx(c)).wait_recv()
    q = qsend[0]
    for d in range(1, nx):
        q = q + qrecv[lax.rem(mx + d, nx)]
    qmat[...] = (q * inv2).astype(bf16)

    bk = min(512, cache)
    length = pick(deal_of, mx, lambda i: jnp.full((1, bk), lengths_ref[i]), (1, bk))
    loads[2].wait()
    maxes[...] = jnp.full(maxes.shape, masked_score, f32)

    def fold_max(h, s):
        m = maxes[h]
        for j in range(s.shape[1] // 128):
            m = jnp.maximum(m, s[:, j * 128:(j + 1) * 128])
        maxes[h] = m

    def score_block(i, carry):
        first = pl.multiple_of(i * bk, bk)
        visible = first + lax.broadcasted_iota(jnp.int32, (1, bk), 1) < length
        for h in range(heads):
            s = lax.dot_general(qmat[:, h * hd:(h + 1) * hd], kc[h, pl.ds(first, bk), :], nt,
                                preferred_element_type=f32)
            s = jnp.where(visible, s, masked_score)
            scores[h, :, pl.ds(first, bk)] = s
            fold_max(h, s)
        return carry

    lax.fori_loop(0, cache // bk, score_block, 0)

    for d in range(1, nx):
        c = lax.rem(mx + d, nx)
        remote(kvsend.at[d], kvrecv.at[c], kv_send.at[d], kv_recv.at[c], atx(c)).wait_recv()
    kv = kvown[...]
    for d in range(1, nx):
        kv = kv + kvrecv[lax.rem(mx + d, nx)].astype(f32)
    kv = (kv * inv).astype(bf16)
    row = lax.rem(lax.broadcasted_iota(jnp.int32, (rows, new), 0), new)
    causal = lax.broadcasted_iota(jnp.int32, (rows, new), 1) <= row
    loads[3].wait()
    unit = hd ** -0.5 * math.log2(math.e)

    def at_copy(h, d, at):
        c = lax.rem(mx + d, nx)
        return remote(agbuf.at[at, h], agbuf.at[at, h], at_send.at[h, d], at_recv.at[h, at], atx(c))

    for h in range(heads):
        fkey[...] = kv[:, h * 2 * hd:h * 2 * hd + hd]
        fval[...] = kv[:, h * 2 * hd + hd:(h + 1) * 2 * hd]
        s = lax.dot_general(qmat[:, h * hd:(h + 1) * hd], fkey[...], nt, preferred_element_type=f32)
        s = jnp.where(causal, s, masked_score)
        fold_max(h, s)
        m = jnp.max(maxes[h], axis=1, keepdims=True)
        w = jnp.exp2((s - m) * unit)
        total = w
        acc = jnp.dot(w.astype(bf16), fval[...], preferred_element_type=f32)

        def weigh(i, carry, h=h, m=m):
            total, acc = carry
            first = pl.multiple_of(i * bk, bk)
            w = jnp.exp2((scores[h, :, pl.ds(first, bk)] - m) * unit)
            for j in range(bk // 128):
                total = total + w[:, j * 128:(j + 1) * 128]
            acc = acc + jnp.dot(w.astype(bf16), vc[h, pl.ds(first, bk), :], preferred_element_type=f32)
            return total, acc

        total, acc = lax.fori_loop(0, cache // bk, weigh, (total, acc))
        agbuf[mx, h] = (acc / jnp.sum(total, axis=1, keepdims=True)).astype(bf16)
        for d in range(1, nx):
            at_copy(h, d, mx).start()

    loads[4].wait()
    tile[...] = jnp.zeros_like(tile)

    def produce(c):
        route = route_of(c)
        rr = jnp.concatenate([route[:, 0:1], route[:, 1:2]], axis=0)
        tile[0:8] = gall[c]
        gate = tile[...].T
        a = [agbuf[c, h] for h in range(heads)]
        a = jnp.concatenate(a, axis=1) if heads > 1 else a[0]
        spread = [jnp.where(rr == float(e), a, jnp.zeros_like(a)) for e in range(experts)]
        y = jnp.dot(jnp.concatenate(spread, axis=1), wo[...], preferred_element_type=f32)
        outs[c] = gate[:, 0:1] * y[0:new] + gate[:, 1:2] * y[new:rows]

    produce(mx)

    def arrive(d, carry):
        c = lax.rem(mx + nx - d, nx)
        t_copy(d, c).wait_recv()
        for h in range(heads):
            at_copy(h, d, c).wait_recv()
        produce(c)
        return carry

    lax.fori_loop(1, nx, arrive, 0)

    def partial(b):
        slot = deal_ref[b // per_req]
        part = pl.ds(pl.multiple_of(lax.rem(b, per_req) * tb, tb), tb)
        return pick(lambda i: i, slot, lambda i: outs[i, part, :], (1, outs.shape[2]))

    def p_copy(z):
        return remote(psend.at[z], precv.at[z], p_send.at[z], p_recv.at[z], aty(partner))

    for d in range(nz - 1, -1, -1):
        z = lax.rem(mz + d, nz)
        psend[z] = partial(z * 2 + 1 - core).astype(bf16)
        p_copy(z).start()

    def z_copy(d, at):
        return remote(zsend.at[d], zrecv.at[at], z_send.at[d], z_recv.at[at],
                      aty(lax.rem(mz + d, nz) * 2 + core))

    for d in range(nz - 1, 0, -1):
        z = lax.rem(mz + d, nz)
        p_copy(z).wait_recv()
        zsend[d] = (partial(z * 2 + core) + precv[z].astype(f32)).astype(bf16)
        z_copy(d, mz).start()
    p_copy(mz).wait_recv()
    total = partial(my) + precv[mz].astype(f32)
    for d in range(1, nz):
        z = lax.rem(mz + nz - d, nz)
        z_copy(d, z).wait_recv()
        total = total + zrecv[z].astype(f32)
    out_ref[...] = total.astype(bf16)

    own.wait_send()
    for d in range(1, nz):
        a_copy(d).wait_send()
        a_in(lax.rem(mz + nz - d, nz) * 2 + core, f_send.at[d]).wait_send()
        z_copy(d, mz).wait_send()
    for z in range(nz):
        p_copy(z).wait_send()
    for d in range(1, nx):
        c = lax.rem(mx + d, nx)
        g_copy(c, d).wait_send()
        q_copy(c, d).wait_send()
        kv_copy(c, d).wait_send()
        t_copy(d, mx).wait_send()
        for h in range(heads):
            at_copy(h, d, mx).wait_send()


def per_device(nx, ny, tokens, gain, w_router, wq, wkv, wo, ck, cv, lengths, deal, route):
    f32, bf16 = jnp.float32, jnp.bfloat16
    tb, width = tokens.shape
    experts, _, heads, hd = wq.shape
    out_w = wo.shape[3]
    cache = ck.shape[2]
    nz = ny // 2
    total = tb * ny
    new = total // nx
    rows = 2 * new
    hw = heads * hd
    dma = pltpu.SemaphoreType.DMA
    vm = pltpu.VMEM
    vspec = pl.BlockSpec(memory_space=pltpu.VMEM)
    sspec = pl.BlockSpec(memory_space=pltpu.SMEM)
    aspec = pl.BlockSpec(memory_space=pl.ANY)
    return pl.pallas_call(
        functools.partial(kernel, nx, ny, width * nx),
        out_shape=jax.ShapeDtypeStruct((tb, out_w), bf16),
        in_specs=[vspec] * 4 + [sspec] * 2 + [aspec] * 5,
        out_specs=vspec,
        scratch_shapes=[
            vm((total, width), bf16),
            vm((experts, width, heads, hd), bf16),
            vm((width, heads, 2 * hd), bf16),
            vm((experts, width, hw), bf16),
            vm((width, 2 * hw), bf16),
            vm((experts * hw, out_w), bf16),
            vm((heads, cache, hd), bf16),
            vm((heads, cache, hd), bf16),
            vm((nx, new, 128), f32),
            vm((nx, rows, hw), f32),
            vm((nx, rows, hw), f32),
            vm((nx, 16, new), f32),
            vm((nx, 16, new), f32),
            vm((nx, new, 2 * hw), bf16),
            vm((nx, new, 2 * hw), bf16),
            vm((new, 2 * hw), f32),
            vm((new, 128), f32),
            vm((nx, 8, new), f32),
            vm((rows, hw), bf16),
            vm((heads, rows, cache), f32),
            vm((heads, rows, 128), f32),
            vm((new, hd), bf16),
            vm((new, hd), bf16),
            vm((nx, heads, rows, hd), bf16),
            vm((nx, new, out_w), f32),
            vm((nz, tb, out_w), bf16),
            vm((nz, tb, out_w), bf16),
            vm((nz, tb, out_w), bf16),
            vm((nz, tb, out_w), bf16),
            dma((5,)), dma((nz,)), dma((ny,)), dma((nz,)),
            dma((nx,)), dma((nx,)), dma((nx,)), dma((nx,)), dma((nx,)), dma((nx,)),
            dma((nx,)), dma((nx,)), dma((heads, nx)), dma((heads, nx)),
            dma((nz,)), dma((nz,)), dma((nz,)), dma((nz,)),
        ],
        compiler_params=pltpu.CompilerParams(
            collective_id=0, has_side_effects=True, vmem_limit_bytes=60 * 1024 * 1024
        ),
    )(
        tokens, gain, w_router.T, route.T, lengths, deal,
        wq, wkv,
        wo.reshape(experts * hw, out_w), ck[0], cv[0],
    )


def solution(mesh):
    placed = (
        P("gy", "gx"), P("gx"), P("gx", None), P(None, "gx", "gy", None), P("gx", "gy", None),
        P(None, "gy", None, "gx"), P("gx", "gy", None, None), P("gx", "gy", None, None),
        P(), P(), P(),
    )
    return jax.shard_map(
        functools.partial(per_device, mesh.shape["gx"], mesh.shape["gy"]),
        mesh=mesh, in_specs=placed, out_specs=P("gy", "gx"), check_vma=False,
    )
```

```python
import functools
import math

import jax
import jax.numpy as jnp
from jax import lax
from jax.experimental import pallas as pl
from jax.experimental.pallas import tpu as pltpu
from jax.sharding import PartitionSpec as P

MESH = pl.DeviceIdType.MESH
masked_score = -1e30
norm_eps = 1e-06


def kernel(
    nx, ny, full_width,
    tokens_ref, gain_ref, wr_ref, route_ref, lengths_ref, deal_ref,
    wq_hbm, wkv_hbm, wo_hbm, k_hbm, v_hbm,
    out_ref,
    xg, wq4, wkv3, wq, wkv, wo, kc, vc, rcol,
    qsend, qrecv, gsend, grecv, kvsend, kvrecv, kvown, tile, gall,
    qmat, scores, maxes, fkey, fval, agbuf, outs, psend, precv, zsend, zrecv,
    ld_sem, a_send, a_recv, f_send, q_send, q_recv, g_send, g_recv, kv_send, kv_recv,
    t_send, t_recv, at_send, at_recv, p_send, p_recv, z_send, z_recv,
):
    f32, bf16 = jnp.float32, jnp.bfloat16
    nt = (((1,), (1,)), ((), ()))
    mx, my = lax.axis_index("gx"), lax.axis_index("gy")
    nz = ny // 2
    mz, core = my // 2, lax.rem(my, 2)
    partner = my + 1 - 2 * core
    tb = tokens_ref.shape[0]
    experts = wq.shape[0]
    heads, cache, hd = kc.shape
    new = xg.shape[0] // nx
    rows = 2 * new
    per_req = new // tb

    def remote(src, dst, ss, rs, dev):
        return pltpu.make_async_remote_copy(
            src_ref=src, dst_ref=dst, send_sem=ss, recv_sem=rs, device_id=dev, device_id_type=MESH
        )

    def atx(c):
        return (c, my)

    def aty(c):
        return (mx, c)

    loads = [
        pltpu.make_async_copy(s, d, ld_sem.at[i])
        for i, (s, d) in enumerate(
            ((wq_hbm, wq4), (wkv_hbm, wkv3), (k_hbm, kc), (v_hbm, vc), (wo_hbm, wo))
        )
    ]
    for load in loads:
        load.start()

    barrier = pltpu.get_barrier_semaphore()
    for d in range(1, nx):
        pl.semaphore_signal(barrier, inc=1, device_id=atx(lax.rem(mx + d, nx)), device_id_type=MESH)
    pl.semaphore_signal(barrier, inc=1, device_id=aty(partner), device_id_type=MESH)
    for d in range(1, nz):
        pl.semaphore_signal(
            barrier, inc=1, device_id=aty(lax.rem(mz + d, nz) * 2 + core), device_id_type=MESH
        )
    pl.semaphore_wait(barrier, nx - 1 + nz)

    def block(b):
        return xg.at[pl.ds(pl.multiple_of(b * tb, tb), tb)]

    def a_copy(d):
        return remote(tokens_ref, block(my), a_send.at[d], a_recv.at[my],
                      aty(lax.rem(mz + d, nz) * 2 + core))

    def a_in(b, ss):
        return remote(block(b), block(b), ss, a_recv.at[b], aty(partner))

    for d in range(1, nz):
        a_copy(d).start()
    own = remote(tokens_ref, block(my), a_send.at[0], a_recv.at[my], aty(partner))
    own.start()
    block(my)[...] = tokens_ref[...]
    def pick(keys, wanted, values, shape):
        acc = values(0)
        for i in range(1, nx):
            acc = jnp.where(jnp.full(shape, keys(i) - wanted) == 0, values(i), acc)
        return acc

    def deal_of(i):
        return deal_ref[i]

    def route_of(c):
        return rcol[c]

    tile[...] = jnp.zeros_like(tile)
    gain = gain_ref[...].astype(f32).reshape(1, gain_ref.shape[0])

    def route_column(c, carry):
        slots = route_ref.shape[0]
        tile[0:slots] = pick(
            deal_of, c, lambda i: route_ref[:, i * new:(i + 1) * new].astype(f32), (slots, new)
        )
        rcol[c] = tile[...].T
        return carry

    lax.fori_loop(0, nx, route_column, 0)
    loads[0].wait()

    def relayout(e, carry):
        for h in range(heads):
            wq[e, :, h * hd:(h + 1) * hd] = wq4[e, :, h, :]
        return carry

    lax.fori_loop(0, experts, relayout, 0)

    for d in range(1, nz):
        b = lax.rem(mz + nz - d, nz) * 2 + core
        c = a_in(b, f_send.at[d])
        c.wait_recv()
        c.start()
    a_in(partner, f_send.at[0]).wait_recv()
    for d in range(1, nz):
        b = lax.rem(mz + nz - d, nz) * 2 + 1 - core
        a_in(b, f_send.at[d]).wait_recv()

    def scaled_of(c):
        x = pick(deal_of, c, lambda i: xg[i * new:(i + 1) * new, :].astype(f32), (1, xg.shape[1]))
        return x, (x * gain).astype(bf16)

    def q_copy(c, d):
        return remote(qsend.at[d], qrecv.at[mx], q_send.at[d], q_recv.at[mx], atx(c))

    def g_copy(c, d):
        return remote(gsend.at[d], grecv.at[mx], g_send.at[d], g_recv.at[mx], atx(c))

    def kv_copy(c, d):
        return remote(kvsend.at[d], kvrecv.at[mx], kv_send.at[d], kv_recv.at[mx], atx(c))

    def project(c):
        x, xs = scaled_of(c)
        route = route_of(c)
        r0, r1 = route[:, 0:1], route[:, 1:2]
        q0 = jnp.zeros((new, heads * hd), f32)
        q1 = q0
        for e in range(experts):
            y = jnp.dot(xs, wq[e], preferred_element_type=f32)
            q0 = jnp.where(r0 == float(e), y, q0)
            q1 = jnp.where(r1 == float(e), y, q1)
        tile[:, 0:experts] = lax.dot_general(xs, wr_ref[...], nt, preferred_element_type=f32)
        tile[:, experts:experts + 1] = jnp.sum(x * x, axis=1, keepdims=True)
        return q0, q1, tile[...].T[0:16]

    def send_q(d, carry):
        c = lax.rem(mx + d, nx)
        q0, q1, g = project(c)
        qsend[d, 0:new] = q0
        qsend[d, new:rows] = q1
        gsend[d] = g
        g_copy(c, d).start()
        q_copy(c, d).start()
        return carry

    lax.fori_loop(1, nx, send_q, 0)
    q0, q1, g = project(mx)
    qsend[0, 0:new] = q0
    qsend[0, new:rows] = q1
    gsend[0] = g
    loads[1].wait()
    for h in range(heads):
        wkv[:, h * 2 * hd:(h + 1) * 2 * hd] = wkv3[:, h, :]

    def send_kv(d, carry):
        c = lax.rem(mx + d, nx)
        kvsend[d] = jnp.dot(scaled_of(c)[1], wkv[...], preferred_element_type=f32).astype(bf16)
        kv_copy(c, d).start()
        return carry

    lax.fori_loop(1, nx, send_kv, 0)
    kvown[...] = jnp.dot(scaled_of(mx)[1], wkv[...], preferred_element_type=f32)

    for d in range(1, nx):
        c = lax.rem(mx + d, nx)
        remote(gsend.at[d], grecv.at[c], g_send.at[d], g_recv.at[c], atx(c)).wait_recv()
    g = gsend[0]
    for d in range(1, nx):
        g = g + grecv[lax.rem(mx + d, nx)]
    tile[...] = jnp.zeros_like(tile)
    tile[0:16] = g
    cols = tile[...].T
    inv = lax.rsqrt(cols[:, experts:experts + 1] * (1.0 / full_width) + norm_eps)
    inv2 = jnp.concatenate([inv, inv], axis=0)
    route = route_of(mx)
    lane = lax.broadcasted_iota(jnp.int32, (new, 128), 1).astype(f32)
    logits = cols * inv
    c0 = jnp.sum(jnp.where(lane == route[:, 0:1], logits, 0.0), axis=1, keepdims=True)
    c1 = jnp.sum(jnp.where(lane == route[:, 1:2], logits, 0.0), axis=1, keepdims=True)
    g0 = jax.nn.sigmoid(c0 - c1).astype(bf16).astype(f32)
    g1 = jax.nn.sigmoid(c1 - c0).astype(bf16).astype(f32)
    gall[mx] = jnp.where(lane == 0, g0, jnp.where(lane == 1, g1, 0.0)).T[0:8]

    def t_copy(d, at):
        c = lax.rem(mx + d, nx)
        return remote(gall.at[at], gall.at[at], t_send.at[d], t_recv.at[at], atx(c))

    for d in range(1, nx):
        t_copy(d, mx).start()

    for d in range(1, nx):
        c = lax.rem(mx + d, nx)
        remote(qsend.at[d], qrecv.at[c], q_send.at[d], q_recv.at[c], atx(c)).wait_recv()
    q = qsend[0]
    for d in range(1, nx):
        q = q + qrecv[lax.rem(mx + d, nx)]
    qmat[...] = (q * inv2).astype(bf16)

    bk = min(512, cache)
    length = pick(deal_of, mx, lambda i: jnp.full((1, bk), lengths_ref[i]), (1, bk))
    loads[2].wait()
    maxes[...] = jnp.full(maxes.shape, masked_score, f32)

    def fold_max(h, s):
        m = maxes[h]
        for j in range(s.shape[1] // 128):
            m = jnp.maximum(m, s[:, j * 128:(j + 1) * 128])
        maxes[h] = m

    def score_block(i, carry):
        first = pl.multiple_of(i * bk, bk)
        visible = first + lax.broadcasted_iota(jnp.int32, (1, bk), 1) < length
        for h in range(heads):
            s = lax.dot_general(qmat[:, h * hd:(h + 1) * hd], kc[h, pl.ds(first, bk), :], nt,
                                preferred_element_type=f32)
            s = jnp.where(visible, s, masked_score)
            scores[h, :, pl.ds(first, bk)] = s
            fold_max(h, s)
        return carry

    lax.fori_loop(0, cache // bk, score_block, 0)

    for d in range(1, nx):
        c = lax.rem(mx + d, nx)
        remote(kvsend.at[d], kvrecv.at[c], kv_send.at[d], kv_recv.at[c], atx(c)).wait_recv()
    kv = kvown[...]
    for d in range(1, nx):
        kv = kv + kvrecv[lax.rem(mx + d, nx)].astype(f32)
    kv = (kv * inv).astype(bf16)
    row = lax.rem(lax.broadcasted_iota(jnp.int32, (rows, new), 0), new)
    causal = lax.broadcasted_iota(jnp.int32, (rows, new), 1) <= row
    loads[3].wait()
    unit = hd ** -0.5 * math.log2(math.e)

    def at_copy(h, d, at):
        c = lax.rem(mx + d, nx)
        return remote(agbuf.at[at, h], agbuf.at[at, h], at_send.at[h, d], at_recv.at[h, at], atx(c))

    for h in range(heads):
        fkey[...] = kv[:, h * 2 * hd:h * 2 * hd + hd]
        fval[...] = kv[:, h * 2 * hd + hd:(h + 1) * 2 * hd]
        s = lax.dot_general(qmat[:, h * hd:(h + 1) * hd], fkey[...], nt, preferred_element_type=f32)
        s = jnp.where(causal, s, masked_score)
        fold_max(h, s)
        m = jnp.max(maxes[h], axis=1, keepdims=True)
        w = jnp.exp2((s - m) * unit)
        total = w
        acc = jnp.dot(w.astype(bf16), fval[...], preferred_element_type=f32)

        def weigh(i, carry, h=h, m=m):
            total, acc = carry
            first = pl.multiple_of(i * bk, bk)
            w = jnp.exp2((scores[h, :, pl.ds(first, bk)] - m) * unit)
            for j in range(bk // 128):
                total = total + w[:, j * 128:(j + 1) * 128]
            acc = acc + jnp.dot(w.astype(bf16), vc[h, pl.ds(first, bk), :], preferred_element_type=f32)
            return total, acc

        total, acc = lax.fori_loop(0, cache // bk, weigh, (total, acc))
        agbuf[mx, h] = (acc / jnp.sum(total, axis=1, keepdims=True)).astype(bf16)
        for d in range(1, nx):
            at_copy(h, d, mx).start()

    loads[4].wait()
    tile[...] = jnp.zeros_like(tile)

    def produce(c):
        route = route_of(c)
        rr = jnp.concatenate([route[:, 0:1], route[:, 1:2]], axis=0)
        tile[0:8] = gall[c]
        gate = tile[...].T
        a = [agbuf[c, h] for h in range(heads)]
        a = jnp.concatenate(a, axis=1) if heads > 1 else a[0]
        spread = [jnp.where(rr == float(e), a, jnp.zeros_like(a)) for e in range(experts)]
        y = jnp.dot(jnp.concatenate(spread, axis=1), wo[...], preferred_element_type=f32)
        outs[c] = gate[:, 0:1] * y[0:new] + gate[:, 1:2] * y[new:rows]

    produce(mx)

    def arrive(d, carry):
        c = lax.rem(mx + nx - d, nx)
        t_copy(d, c).wait_recv()
        for h in range(heads):
            at_copy(h, d, c).wait_recv()
        produce(c)
        return carry

    lax.fori_loop(1, nx, arrive, 0)

    def partial(b):
        slot = deal_ref[b // per_req]
        part = pl.ds(pl.multiple_of(lax.rem(b, per_req) * tb, tb), tb)
        return pick(lambda i: i, slot, lambda i: outs[i, part, :], (1, outs.shape[2]))

    def p_copy(z):
        return remote(psend.at[z], precv.at[z], p_send.at[z], p_recv.at[z], aty(partner))

    for d in range(nz - 1, -1, -1):
        z = lax.rem(mz + d, nz)
        psend[z] = partial(z * 2 + 1 - core).astype(bf16)
        p_copy(z).start()

    def z_copy(d, at):
        return remote(zsend.at[d], zrecv.at[at], z_send.at[d], z_recv.at[at],
                      aty(lax.rem(mz + d, nz) * 2 + core))

    for d in range(nz - 1, 0, -1):
        z = lax.rem(mz + d, nz)
        p_copy(z).wait_recv()
        zsend[d] = (partial(z * 2 + core) + precv[z].astype(f32)).astype(bf16)
        z_copy(d, mz).start()
    p_copy(mz).wait_recv()
    total = partial(my) + precv[mz].astype(f32)
    for d in range(1, nz):
        z = lax.rem(mz + nz - d, nz)
        z_copy(d, z).wait_recv()
        total = total + zrecv[z].astype(f32)
    out_ref[...] = total.astype(bf16)

    own.wait_send()
    for d in range(1, nz):
        a_copy(d).wait_send()
        a_in(lax.rem(mz + nz - d, nz) * 2 + core, f_send.at[d]).wait_send()
        z_copy(d, mz).wait_send()
    for z in range(nz):
        p_copy(z).wait_send()
    for d in range(1, nx):
        c = lax.rem(mx + d, nx)
        g_copy(c, d).wait_send()
        q_copy(c, d).wait_send()
        kv_copy(c, d).wait_send()
        t_copy(d, mx).wait_send()
        for h in range(heads):
            at_copy(h, d, mx).wait_send()


def per_device(nx, ny, tokens, gain, w_router, wq, wkv, wo, ck, cv, lengths, deal, route):
    f32, bf16 = jnp.float32, jnp.bfloat16
    tb, width = tokens.shape
    experts, _, heads, hd = wq.shape
    out_w = wo.shape[3]
    cache = ck.shape[2]
    nz = ny // 2
    total = tb * ny
    new = total // nx
    rows = 2 * new
    hw = heads * hd
    dma = pltpu.SemaphoreType.DMA
    vm = pltpu.VMEM
    vspec = pl.BlockSpec(memory_space=pltpu.VMEM)
    sspec = pl.BlockSpec(memory_space=pltpu.SMEM)
    aspec = pl.BlockSpec(memory_space=pl.ANY)
    return pl.pallas_call(
        functools.partial(kernel, nx, ny, width * nx),
        out_shape=jax.ShapeDtypeStruct((tb, out_w), bf16),
        in_specs=[vspec] * 4 + [sspec] * 2 + [aspec] * 5,
        out_specs=vspec,
        scratch_shapes=[
            vm((total, width), bf16),
            vm((experts, width, heads, hd), bf16),
            vm((width, heads, 2 * hd), bf16),
            vm((experts, width, hw), bf16),
            vm((width, 2 * hw), bf16),
            vm((experts * hw, out_w), bf16),
            vm((heads, cache, hd), bf16),
            vm((heads, cache, hd), bf16),
            vm((nx, new, 128), f32),
            vm((nx, rows, hw), f32),
            vm((nx, rows, hw), f32),
            vm((nx, 16, new), f32),
            vm((nx, 16, new), f32),
            vm((nx, new, 2 * hw), bf16),
            vm((nx, new, 2 * hw), bf16),
            vm((new, 2 * hw), f32),
            vm((new, 128), f32),
            vm((nx, 8, new), f32),
            vm((rows, hw), bf16),
            vm((heads, rows, cache), f32),
            vm((heads, rows, 128), f32),
            vm((new, hd), bf16),
            vm((new, hd), bf16),
            vm((nx, heads, rows, hd), bf16),
            vm((nx, new, out_w), f32),
            vm((nz, tb, out_w), bf16),
            vm((nz, tb, out_w), bf16),
            vm((nz, tb, out_w), bf16),
            vm((nz, tb, out_w), bf16),
            dma((5,)), dma((nz,)), dma((ny,)), dma((nz,)),
            dma((nx,)), dma((nx,)), dma((nx,)), dma((nx,)), dma((nx,)), dma((nx,)),
            dma((nx,)), dma((nx,)), dma((heads, nx)), dma((heads, nx)),
            dma((nz,)), dma((nz,)), dma((nz,)), dma((nz,)),
        ],
        compiler_params=pltpu.CompilerParams(
            collective_id=0, has_side_effects=True, vmem_limit_bytes=60 * 1024 * 1024
        ),
    )(
        tokens, gain, w_router.T, route.T, lengths, deal,
        wq, wkv,
        wo.reshape(experts * hw, out_w), ck[0], cv[0],
    )


def solution(mesh):
    placed = (
        P("gy", "gx"), P("gx"), P("gx", None), P(None, "gx", "gy", None), P("gx", "gy", None),
        P(None, "gy", None, "gx"), P("gx", "gy", None, None), P("gx", "gy", None, None),
        P(), P(), P(),
    )
    return jax.shard_map(
        functools.partial(per_device, mesh.shape["gx"], mesh.shape["gy"]),
        mesh=mesh, in_specs=placed, out_specs=P("gy", "gx"), check_vma=False,
    )
```
